32 devices in a mesh: chip: 2 (over core), row: 4 (over y, x), grp: 4 (over z).
Axes of the slice: x: 2, y: 2, z: 4, core: 2. Of those that a mesh axis runs over, the one named last changes fastest.
Arguments:
- old_velocity: float32 [2, 1024, 2048], P(None, 'row', ('chip', 'grp')), may hold values from -6 to 6
- surface_stress: float32 [2, 1024, 2048], P(None, 'row', ('chip', 'grp')), may hold values from -6 to 6
- mass_term: float32 [1024, 2048], P('row', ('chip', 'grp')), may hold values from 0.2 to 2
- ocean_drag: float32 [1024, 2048], P('row', ('chip', 'grp')), may hold values from 0.1 to 1
- strength: float32 [1024, 2048], P('row', ('chip', 'grp')), may hold values from 1 to 10
- ice_mask: int32 [1024, 2048], P('row', ('chip', 'grp')), may hold values from 0 to 1, as said below
- ocean_mask: int32 [1024, 2048], P('row', ('chip', 'grp')), may hold values 0 or 1
- ice_blocks: int32 [8, 8], P(('chip', 'grp')), may hold values from 0 to 15, as said below
Outputs:
- new_velocity: float32 [2, 1024, 2048], P(None, 'row', ('chip', 'grp'))
The draws below stay inside these ranges and needn't reach their ends.
Inputs may be any that keep to these rules, and one draw needn't show every extreme that they name: `ice_blocks`: entry n of row c names block n % 4 (row-major over the blocks of 128 x 128 cells of a tile) of tile row n // 4 in tile column c. Each row lists 8 different blocks; the blocks of one tile stand together, tiles with more listed blocks first; all 4 blocks of the last tile row of every column are listed. The entry at place k of a row is owned by tile row k % 4 of that column, as its block number k // 4. `ice_mask`: ice lies only in cells of the blocks listed in ice_blocks.
All inputs are finite; a program needn't handle non-finite values. No bound on the sum of `ocean_mask` on one device may be relied on, other than what follows from the above.
Results may differ from the reference program's by a relative error of at most 0.00011.
Values sent between devices are 32-bit elements; how exact they have to be, the bound alone decides.
A program may use at most 128 MiB of HBM per device.

```python
import math
import jax
import jax.numpy as jnp

BS = 128
TX = 256
TY = 256
KRYLOV = 2
CYCLES = 2
SWEEPS = 2
BLOCKS_TILE = 4
SLOTS = 2
NCOL = 8
NX = 1024
NY = 2048
N_ROW = 4


def column_plan(key, column):
    column_key = jax.random.fold_in(jax.random.fold_in(key, 7), column)
    key_tiles, key_blocks, key_order = jax.random.split(column_key, 3)
    total_blocks = N_ROW * BLOCKS_TILE
    block_ids = jnp.arange(total_blocks, dtype=jnp.int32)
    tile_of = block_ids // BLOCKS_TILE
    weights = jax.random.randint(key_tiles, (N_ROW,), 0, 4)
    weights = jnp.where(jnp.arange(N_ROW) == N_ROW - 1, 8, weights)
    noise = jax.random.randint(key_blocks, (total_blocks,), 0, 4096)
    score = (weights[tile_of] * 4096 + noise) * total_blocks + block_ids
    chosen = jnp.argsort(-score)[:N_ROW * SLOTS]
    is_icy = jnp.zeros((total_blocks,), jnp.int32).at[chosen].set(1)
    counts = jnp.sum(is_icy.reshape(N_ROW, BLOCKS_TILE), axis=1)
    tie_rank = jnp.argsort(jax.random.permutation(key_order, N_ROW)).astype(jnp.int32)
    deal_key = ((BLOCKS_TILE - counts[tile_of]) * N_ROW + tie_rank[tile_of]) * BLOCKS_TILE + block_ids % BLOCKS_TILE
    deal_key = deal_key + (1 - is_icy) * (BLOCKS_TILE + 1) * N_ROW * BLOCKS_TILE
    dealt = jnp.argsort(deal_key)[:N_ROW * SLOTS].astype(jnp.int32)
    return (dealt, is_icy)


def draw_ice_blocks(key, part):
    lists, flags = jax.vmap(lambda column: column_plan(key, column))(jnp.arange(NCOL, dtype=jnp.int32))
    return lists.astype(jnp.int32)


def draw_ice_mask(key, part):
    lists, flags = jax.vmap(lambda column: column_plan(key, column))(jnp.arange(NCOL, dtype=jnp.int32))
    shaped = flags.reshape(NCOL, N_ROW, TX // BS, TY // BS)
    shaped = jnp.repeat(jnp.repeat(shaped, BS, axis=2), BS, axis=3)
    cells = shaped.transpose(1, 2, 0, 3).reshape(NX, NY)
    random_bits = jax.random.randint(jax.random.fold_in(key, 9), (NX, NY), 0, 8)
    return jnp.where(random_bits > 0, cells, 0).astype(jnp.int32)


def plant(values, key, least, high):
    longest = values.shape.index(max(values.shape))
    spots = []
    for shift in (0, 1):
        where = [jax.random.randint(jax.random.fold_in(key, axis), (), 0, length) for axis, length in enumerate(values.shape)]
        where[longest] = (where[longest] + shift) % values.shape[longest]
        spots.append(tuple(where))
    return values.at[spots[0]].set(least).at[spots[1]].set(high)


def block_scale(own_key, shape, cuts, smallest, largest):
    factor_of, own = 1.0, jax.random.fold_in(own_key, 6)
    for position, shards_of in cuts:
        heights = jnp.exp(jax.random.uniform(jax.random.fold_in(own, position), (shards_of,), jnp.float32, smallest / len(cuts), largest / len(cuts)))
        factor_of = factor_of * jnp.repeat(heights, shape[position] // shards_of).reshape([-1 if axis == position else 1 for axis in range(len(shape))])
    return factor_of


def gaussian(own_key, extent, scale, most, cuts=(), kind=jnp.bfloat16):
    drawn = scale * jax.random.normal(own_key, extent, jnp.float32)
    if cuts:
        drawn = drawn * block_scale(own_key, extent, cuts, -0.22, 0.18)
    return jnp.clip(drawn, -most, most).astype(kind)


def setup_inputs(seed: int = 0) -> dict:
    seeds = jax.random.split(jax.random.key(seed), 9)
    return {
        "old_velocity": gaussian(seeds[0], (2, NX, NY), 1.0, 6.0, ((1, 4), (2, 8)), jnp.float32),
        "surface_stress": gaussian(seeds[1], (2, NX, NY), 1.0, 6.0, ((1, 4), (2, 8)), jnp.float32),
        "mass_term": jnp.clip(jnp.exp(math.log(2.0) - 2.3025851 * jax.random.uniform(seeds[2], (NX, NY), jnp.float32) ** block_scale(seeds[2], (NX, NY), ((0, 4), (1, 8)), -0.2, 0.2)), 0.2, 2.0),
        "ocean_drag": jnp.clip(jnp.exp(math.log(1.0) - 2.3025851 * jax.random.uniform(seeds[3], (NX, NY), jnp.float32) ** block_scale(seeds[3], (NX, NY), ((0, 4), (1, 8)), -0.2, 0.2)), 0.1, 1.0),
        "strength": jnp.clip(jnp.exp(math.log(10.0) - 2.3025851 * jax.random.uniform(seeds[4], (NX, NY), jnp.float32) ** block_scale(seeds[4], (NX, NY), ((0, 4), (1, 8)), -0.2, 0.2)), 1.0, 10.0),
        "ice_mask": draw_ice_mask(jax.random.fold_in(seeds[8], 71), 0),
        "ocean_mask": plant((jax.random.randint(seeds[6], (NX, NY), 0, 10) < 9).astype(jnp.int32), jax.random.fold_in(seeds[6], 1), 0, 1),
        "ice_blocks": draw_ice_blocks(jax.random.fold_in(seeds[8], 71), 0),
    }


RELAX = 0.8
DMIN_SQ = 0.25

def stencil(padded, zeta_field, diag_field):

    def pieces(field):
        center = field[..., 1:-1, 1:-1]
        second_x = field[..., 2:, 1:-1] + field[..., :-2, 1:-1] - 2.0 * center
        second_y = field[..., 1:-1, 2:] + field[..., 1:-1, :-2] - 2.0 * center
        mixed = 0.25 * (field[..., 2:, 2:] - field[..., 2:, :-2] - field[..., :-2, 2:] + field[..., :-2, :-2])
        return (center, second_x, second_y, mixed)
    part_u = pieces(padded[..., 0, :, :])
    part_v = pieces(padded[..., 1, :, :])
    along_u = diag_field * part_u[0] - 1.25 * zeta_field * part_u[1] - 0.25 * zeta_field * part_u[2] - zeta_field * part_v[3]
    along_v = diag_field * part_v[0] - 0.25 * zeta_field * part_v[1] - 1.25 * zeta_field * part_v[2] - zeta_field * part_u[3]
    return jnp.stack([along_u, along_v], axis=-3)

def precondition(vector, zeta_blocks, diag_blocks):
    diagonal_total = (diag_blocks + 3.0 * zeta_blocks)[:, None]
    iterate = vector / diagonal_total
    for relaxation in range(SWEEPS):
        padded = jnp.pad(iterate, ((0, 0), (0, 0), (1, 1), (1, 1)))
        iterate = iterate + RELAX * (vector - stencil(padded, zeta_blocks, diag_blocks)) / diagonal_total
    return iterate

def least_squares(hessenberg, start_norm):
    steps_count = hessenberg.shape[1]
    row_list = [hessenberg[i] for i in range(steps_count + 1)]
    target_vec = [start_norm] + [jnp.zeros((), jnp.float32) for i in range(steps_count)]
    for j in range(steps_count):
        upper = row_list[j][j]
        lower = row_list[j + 1][j]
        radius = jnp.sqrt(upper * upper + lower * lower)
        cosine = upper / radius
        sine_part = lower / radius
        first_row = cosine * row_list[j] + sine_part * row_list[j + 1]
        second_row = -sine_part * row_list[j] + cosine * row_list[j + 1]
        row_list[j], row_list[j + 1] = (first_row, second_row)
        first_val = cosine * target_vec[j] + sine_part * target_vec[j + 1]
        second_val = -sine_part * target_vec[j] + cosine * target_vec[j + 1]
        target_vec[j], target_vec[j + 1] = (first_val, second_val)
    weights_out = [None] * steps_count
    for j in range(steps_count - 1, -1, -1):
        accum = target_vec[j]
        for i in range(j + 1, steps_count):
            accum = accum - row_list[j][i] * weights_out[i]
        weights_out[j] = accum / row_list[j][j]
    return weights_out

def to_blocks(grid):
    channels = grid.shape[0]
    shaped = grid.reshape(channels, NX // BS, BS, NY // BS, BS).transpose(1, 3, 0, 2, 4)
    return shaped.reshape(NX // BS * (NY // BS), channels, BS, BS)

def from_blocks(blocks):
    channels = blocks.shape[1]
    shaped = blocks.reshape(NX // BS, NY // BS, channels, BS, BS).transpose(2, 0, 3, 1, 4)
    return shaped.reshape(channels, NX, NY)

def live_cells(ice_blocks):
    per_row = TY // BS
    tile_row = ice_blocks // BLOCKS_TILE
    inside = ice_blocks % BLOCKS_TILE
    block_row = (tile_row * (TX // BS) + inside // per_row).astype(jnp.int32)
    block_col = (jnp.arange(NCOL, dtype=jnp.int32)[:, None] * per_row + inside % per_row).astype(jnp.int32)
    grid_blocks = jnp.zeros((NX // BS, NY // BS), jnp.float32).at[block_row, block_col].set(1.0)
    return jnp.repeat(jnp.repeat(grid_blocks, BS, axis=0), BS, axis=1)

def reference(old_velocity, surface_stress, mass_term, ocean_drag, strength, ice_mask, ocean_mask, ice_blocks):
    padded = jnp.pad(old_velocity, ((0, 0), (1, 1), (1, 1)))
    flow_u = padded[0]
    flow_v = padded[1]
    strain_xx = 0.5 * (flow_u[2:, 1:-1] - flow_u[:-2, 1:-1])
    strain_yy = 0.5 * (flow_v[1:-1, 2:] - flow_v[1:-1, :-2])
    strain_xy = 0.25 * (flow_u[1:-1, 2:] - flow_u[1:-1, :-2] + flow_v[2:, 1:-1] - flow_v[:-2, 1:-1])
    deform_sq = 1.25 * (strain_xx * strain_xx + strain_yy * strain_yy) + strain_xy * strain_xy + 1.5 * strain_xx * strain_yy
    is_ocean = ocean_mask.astype(jnp.float32)
    zeta_field = is_ocean * ice_mask.astype(jnp.float32) * strength / (2.0 * jnp.sqrt(deform_sq + DMIN_SQ))
    diag_field = is_ocean * (mass_term + ocean_drag) + (1.0 - is_ocean)
    live = live_cells(ice_blocks)
    rhs = live * is_ocean * (surface_stress + mass_term * old_velocity)
    zeta_blocks = to_blocks(zeta_field[None])[:, 0]
    diag_blocks = to_blocks(diag_field[None])[:, 0]

    def system(vector):
        grown = jnp.pad(vector, ((0, 0), (1, 1), (1, 1)))
        return live * stencil(grown, zeta_field, diag_field)

    def apply_precond(vector):
        return from_blocks(precondition(to_blocks(vector), zeta_blocks, diag_blocks))
    solution = jnp.zeros_like(rhs)
    for restart in range(CYCLES):
        if restart == 0:
            residual = rhs
        else:
            residual = rhs - system(solution)
        start_norm = jnp.sqrt(jnp.sum(residual * residual))
        basis_list = [residual / start_norm]
        directions = []
        hessenberg = jnp.zeros((KRYLOV + 1, KRYLOV), jnp.float32)
        for arnoldi in range(KRYLOV):
            direction = apply_precond(basis_list[arnoldi])
            directions.append(direction)
            images = system(direction)
            products = jnp.stack([jnp.sum(images * vector) for vector in basis_list])
            for i in range(arnoldi + 1):
                images = images - products[i] * basis_list[i]
            new_norm = jnp.sqrt(jnp.sum(images * images))
            hessenberg = hessenberg.at[:arnoldi + 1, arnoldi].set(products).at[arnoldi + 1, arnoldi].set(new_norm)
            if arnoldi + 1 < KRYLOV:
                basis_list.append(images / new_norm)
        weights_out = least_squares(hessenberg, start_norm)
        for arnoldi in range(KRYLOV):
            solution = solution + weights_out[arnoldi] * directions[arnoldi]
    return solution
```

```python
import functools

import jax
import jax.numpy as jnp
from jax import lax
from jax.experimental import pallas as pl
from jax.experimental.pallas import tpu as pltpu
from jax.sharding import PartitionSpec as P

MESH = pl.DeviceIdType.MESH
BS = 128
DMIN_SQ = 0.25
STEPS = 4
VEL = STEPS
ROWS_P = 32
ROWS_S = 16
PAD = 8
DIRS = ((-1, 0), (1, 0), (0, 1), (1, 1), (-1, 1), (0, -1), (1, -1), (-1, -1))
PAIRS = [(i, j) for j in range(STEPS + 1) for i in range(j + 1)]
INDEX = {pair: n for n, pair in enumerate(PAIRS)}
COUNT = 16


def neighbour_sum(p, p_n, p_s, q, q_n, q_s):
    tq = q_s - q_n
    tp = p_s - p_n
    p5 = p
    q5 = 5.0 * q
    return (5.0 * (p_n + p_s), p5 + tq, p5 - tq), (q_n + q_s, q5 + tp, q5 - tp)


def scalars(gram):
    n = STEPS + 1

    def g(i, j):
        return gram[INDEX[(min(i, j), max(i, j))]]

    def dot(x, y):
        total = None
        for j in range(n):
            if y[j] is None:
                continue
            inner = None
            for i in range(n):
                if x[i] is None:
                    continue
                term = x[i] * g(i, j)
                inner = term if inner is None else inner + term
            term = inner * y[j]
            total = term if total is None else total + term
        return total

    def shift(x):
        return [None] + x[: n - 1]

    def add(x, y):
        return [b if a is None else a if b is None else a + b for a, b in zip(x, y)]

    def cycle(r):
        w1 = add(r, shift(r))
        w2 = shift(w1)
        b1, b2 = dot(r, w1), dot(r, w2)
        g11, g12, g22 = dot(w1, w1), dot(w1, w2), dot(w2, w2)
        det = g11 * g22 - g12 * g12
        good = det > 0.0
        inv = 1.0 / jnp.where(good, det, 1.0)
        single = jnp.where(g11 > 0.0, b1 / jnp.where(g11 > 0.0, g11, 1.0), 0.0)
        a = jnp.where(good, (b1 * g22 - b2 * g12) * inv, single)
        b = jnp.where(good, (g11 * b2 - g12 * b1) * inv, 0.0)
        return a, b

    one = jnp.ones_like(gram[0])
    a0, b0 = cycle([one, None, None, None, None])
    c = [1.0 - a0, -(a0 + b0), -b0]
    a1, b1 = cycle(c + [None, None])
    return (
        a0 + a1 * c[0],
        b0 + a1 * c[1] + b1 * c[0],
        a1 * c[2] + b1 * c[1],
        b1 * c[2],
    )


def kernel(
    sizes,
    vel_ref,
    stress_ref,
    mass_ref,
    drag_ref,
    strength_ref,
    ice_ref,
    ocean_ref,
    listed_ref,
    out_ref,
    D,
    V,
    Z0,
    Z1,
    CO,
    EB,
    RB,
    HC,
    GB,
    GX,
    R1,
    R2,
    send_sem,
    recv_sem,
    s1,
    r1,
    s2,
    r2,
):
    n_chip, n_row, n_grp, rows, cols = sizes
    n_col = n_chip * n_grp
    nbi, nbj = rows // BS, cols // BS
    chip = lax.axis_index("chip")
    row = lax.axis_index("row")
    grp = lax.axis_index("grp")
    col = chip * n_grp + grp

    def device(dr, dc):
        r = lax.rem(row + (dr + n_row), n_row)
        c = lax.rem(col + (dc + n_col), n_col)
        return (lax.div(c, n_grp), r, lax.rem(c, n_grp))

    partners = list(DIRS)
    for o in range(1, n_row):
        if o not in (1, n_row - 1):
            partners.append((o, 0))
    for o in range(1, n_col):
        if o not in (1, n_col - 1):
            partners.append((0, o))
    barrier = pltpu.get_barrier_semaphore()
    for dr, dc in partners:
        pl.semaphore_signal(barrier, inc=1, device_id=device(dr, dc), device_id_type=MESH)

    has_n = row > 0
    has_s = row < n_row - 1
    has_w = col > 0
    has_e = col < n_col - 1

    lane_p = lax.broadcasted_iota(jnp.int32, (ROWS_P, BS), 1)
    lane_s = lax.broadcasted_iota(jnp.int32, (ROWS_S, BS), 1)
    sub_s = lax.broadcasted_iota(jnp.int32, (ROWS_S, BS), 0)
    eye = lax.broadcasted_iota(jnp.int32, (BS, BS), 0) == lax.broadcasted_iota(jnp.int32, (BS, BS), 1)
    lane_1 = lax.broadcasted_iota(jnp.int32, (1, BS), 1)

    def east(x):
        return pltpu.roll(x, BS - 1, 1)

    def west(x):
        return pltpu.roll(x, 1, 1)

    def copies(slot, dirs):
        found = []
        for d in dirs:
            dr, dc = DIRS[d]
            if dc == 0:
                first, there = (PAD, PAD + rows) if dr < 0 else (rows, 0)
                src = D.at[slot, :, :, pl.ds(first, PAD), :]
                dst = D.at[slot, :, :, pl.ds(there, PAD), :]
            else:
                src = EB.at[slot, 0 if dc > 0 else 1]
                dst = RB.at[slot, d - 2]
            found.append(
                pltpu.make_async_remote_copy(
                    src_ref=src,
                    dst_ref=dst,
                    send_sem=send_sem.at[slot, d],
                    recv_sem=recv_sem.at[slot, d],
                    device_id=device(dr, dc),
                    device_id_type=MESH,
                )
            )
        return found

    def send_halo(slot, dirs):
        for side in range(2):
            bj, lane = (nbj - 1, BS - 1) if side == 0 else (0, 0)
            lines = []
            for comp in range(2):
                for bi in range(nbi):
                    x = D[slot, comp, bj, pl.ds(PAD + bi * BS, BS), :]
                    edge = jnp.broadcast_to(x[:, lane : lane + 1], (BS, BS))
                    lines.append(jnp.sum(jnp.where(eye, edge, 0.0), axis=0, keepdims=True))
            lines.append(jnp.zeros((8 - 2 * nbi, BS), jnp.float32))
            EB[slot, side] = jnp.concatenate(lines, axis=0)
        moved = copies(slot, dirs)
        for copy in moved:
            copy.start()
        return moved

    def take_halo(slot, moved, with_corners):
        for copy in moved:
            copy.wait_recv()
        for comp in range(2):
            for bj in range(nbj):
                top = D[slot, comp, bj, 0:PAD, :]
                D[slot, comp, bj, 0:PAD, :] = jnp.where(has_n, top, 0.0)
                low = D[slot, comp, bj, PAD + rows : PAD + rows + PAD, :]
                D[slot, comp, bj, PAD + rows : PAD + rows + PAD, :] = jnp.where(has_s, low, 0.0)
        for side in range(2):
            present = has_w if side == 0 else has_e
            block = RB[slot, 3 * side]
            lines = [[block[c * nbi + b : c * nbi + b + 1] for b in range(nbi)] for c in range(2)]
            if not with_corners:
                for c in range(2):
                    for b in range(nbi):
                        HC[side, c * nbi + b : c * nbi + b + 1, :] = jnp.where(present, lines[c][b], 0.0)
                continue
            above = RB[slot, 3 * side + 1]
            below = RB[slot, 3 * side + 2]
            steps = []
            for c in range(2):
                line = []
                for b in range(nbi):
                    up = west(lines[c][b - 1]) if b > 0 else jnp.where(has_n, west(above[c * nbi + nbi - 1 : c * nbi + nbi]), 0.0)
                    down = east(lines[c][b + 1]) if b < nbi - 1 else jnp.where(has_s, east(below[c * nbi : c * nbi + 1]), 0.0)
                    north = jnp.where(lane_1 == 0, up, west(lines[c][b]))
                    south = jnp.where(lane_1 == BS - 1, down, east(lines[c][b]))
                    line.append(south - north)
                steps.append(line)
            sign = -1.0 if side == 0 else 1.0
            for b in range(nbi):
                HC[side, b : b + 1, :] = jnp.where(present, lines[0][b] + sign * steps[1][b], 0.0)
                HC[side, nbi + b : nbi + b + 1, :] = jnp.where(present, 5.0 * lines[1][b] + sign * steps[0][b], 0.0)

    def halo_column(side, comp, bi, r0):
        line = HC[side, pl.ds(comp * nbi + bi, 1), :]
        kept = jnp.where(lane_s == sub_s + r0, jnp.broadcast_to(line, (ROWS_S, BS)), 0.0)
        return jnp.sum(kept, axis=1, keepdims=True)

    def fold(x):
        total = x[0:8]
        for n in range(1, ROWS_S // 8):
            total = total + x[8 * n : 8 * n + 8]
        return total

    for comp in range(2):
        for bj in range(nbj):
            D[VEL, comp, bj, PAD : PAD + rows, :] = vel_ref[comp, :, bj * BS : (bj + 1) * BS]
    pl.semaphore_wait(barrier, len(partners))
    vel_dirs = (0, 1, 2, 5)
    pending = [send_halo(VEL, vel_dirs)]
    for Z in (Z0, Z1):
        for comp in range(2):
            for b in range(nbi * nbj):
                Z[comp, b, 0:PAD, :] = jnp.zeros((PAD, BS), jnp.float32)
                Z[comp, b, PAD + BS : PAD + BS + PAD, :] = jnp.zeros((PAD, BS), jnp.float32)
    live = []
    for b in range(nbi * nbj):
        wanted = row * (nbi * nbj) + b
        flag = jnp.float32(0.0)
        for n in range(listed_ref.shape[1]):
            flag = jnp.maximum(flag, jnp.where(listed_ref[0, n] == wanted, 1.0, 0.0))
        live.append(flag)
    take_halo(VEL, pending[0], False)

    per_block = BS // ROWS_S
    zero8 = jnp.zeros((8, BS), jnp.float32)

    def setup(t, acc):
        bi = lax.div(t, per_block)
        r0 = lax.rem(t, per_block) * ROWS_S
        start = pl.multiple_of(t * ROWS_S, ROWS_S)
        here = pl.ds(start, ROWS_S)
        us, vs = [], []
        for bj in range(nbj):
            us.append([D[VEL, 0, bj, pl.ds(PAD + start + d, ROWS_S), :] for d in (-1, 0, 1)])
            vs.append([D[VEL, 1, bj, pl.ds(PAD + start + d, ROWS_S), :] for d in (-1, 0, 1)])

        def across(parts, comp):
            e = [east(x[1]) for x in parts]
            w = [west(x[1]) for x in parts]
            edge_e, edge_w = halo_column(1, comp, bi, r0), halo_column(0, comp, bi, r0)
            found = []
            for bj in range(nbj):
                right = e[bj + 1] if bj < nbj - 1 else edge_e
                left = w[bj - 1] if bj > 0 else edge_w
                found.append(jnp.where(lane_s == BS - 1, right, e[bj]) - jnp.where(lane_s == 0, left, w[bj]))
            return found

        du, dv = across(us, 0), across(vs, 1)
        for bj in range(nbj):
            lanes = slice(bj * BS, (bj + 1) * BS)
            e11 = 0.5 * (us[bj][2] - us[bj][0])
            e22 = 0.5 * dv[bj]
            e12 = 0.25 * (du[bj] + vs[bj][2] - vs[bj][0])
            deform = 1.25 * (e11 * e11 + e22 * e22) + e12 * e12 + 1.5 * e11 * e22
            ocean = ocean_ref[here, lanes].astype(jnp.float32)
            ice = ice_ref[here, lanes].astype(jnp.float32)
            mass = mass_ref[here, lanes]
            zeta = ocean * ice * strength_ref[here, lanes] / (2.0 * jnp.sqrt(deform + DMIN_SQ))
            total = ocean * (mass + drag_ref[here, lanes]) + (1.0 - ocean) + 3.0 * zeta
            inv = 1.0 / total
            flag = live[bj]
            for b in range(1, nbi):
                flag = jnp.where(bi == b, live[b * nbj + bj], flag)
            scaled = ocean * flag
            CO[0, bj, here, :] = inv
            CO[1, bj, here, :] = 0.2 * zeta * inv
            CO[2, bj, here, :] = flag * total
            CO[3, bj, here, :] = flag * (0.25 * zeta)
            for comp in range(2):
                vel = us[bj][1] if comp == 0 else vs[bj][1]
                rhs = scaled * (stress_ref[comp, here, lanes] + mass * vel)
                V[0, comp, bj, here, :] = rhs
                Z0[comp, bi * nbj + bj, pl.ds(PAD + r0, ROWS_S), :] = rhs * inv
                acc = acc + fold(rhs * rhs)
        return acc

    def put_products(step, values):
        for i, value in enumerate(values):
            n = INDEX[(i, step)]
            GB[n : n + 1, :] = jnp.sum(value, axis=0, keepdims=True)

    GB[COUNT - 1 : COUNT, :] = jnp.zeros((1, BS), jnp.float32)
    put_products(0, [lax.fori_loop(0, rows // ROWS_S, setup, zero8)])

    def block_sums(Z, b, c):
        first = PAD + c * ROWS_P
        p = [Z[0, b, pl.ds(first + d, ROWS_P), :] for d in (-1, 0, 1)]
        q = [Z[1, b, pl.ds(first + d, ROWS_P), :] for d in (-1, 0, 1)]
        sums = []
        for base, ye, yw in neighbour_sum(p[1], p[0], p[2], q[1], q[0], q[2]):
            e = jnp.where(lane_p == BS - 1, 0.0, east(ye))
            w = jnp.where(lane_p == 0, 0.0, west(yw))
            sums.append(base + e + w)
        return (p[1], q[1]), sums

    def sweep(slot):
        def first(b, carry):
            bi, bj = lax.div(b, nbj), lax.rem(b, nbj)
            for c in range(BS // ROWS_P):
                z, sums = block_sums(Z0, b, c)
                k = CO[1, bj, pl.ds(pl.multiple_of(bi * BS, BS) + c * ROWS_P, ROWS_P), :]
                for comp in range(2):
                    Z1[comp, b, PAD + c * ROWS_P : PAD + (c + 1) * ROWS_P, :] = z[comp] + k * sums[comp]
            return carry

        def second(b, carry):
            bi, bj = lax.div(b, nbj), lax.rem(b, nbj)
            for c in range(BS // ROWS_P):
                z, sums = block_sums(Z1, b, c)
                at = pl.multiple_of(bi * BS, BS) + c * ROWS_P
                k = CO[1, bj, pl.ds(at, ROWS_P), :]
                for comp in range(2):
                    z0 = Z0[comp, b, PAD + c * ROWS_P : PAD + (c + 1) * ROWS_P, :]
                    D[slot, comp, bj, pl.ds(PAD + at, ROWS_P), :] = 0.2 * z[comp] + 0.8 * z0 + k * sums[comp]
            return carry

        lax.fori_loop(0, nbi * nbj, first, 0)
        lax.fori_loop(0, nbi * nbj, second, 0)

    def operator(step):
        last = step == STEPS - 1

        def body(t, acc):
            acc = list(acc)
            bi = lax.div(t, per_block)
            r0 = lax.rem(t, per_block) * ROWS_S
            start = pl.multiple_of(t * ROWS_S, ROWS_S)
            here = pl.ds(start, ROWS_S)
            z, base, es, ws = [], [], [[], []], [[], []]
            for bj in range(nbj):
                p = [D[step, 0, bj, pl.ds(PAD + start + d, ROWS_S), :] for d in (-1, 0, 1)]
                q = [D[step, 1, bj, pl.ds(PAD + start + d, ROWS_S), :] for d in (-1, 0, 1)]
                parts = neighbour_sum(p[1], p[0], p[2], q[1], q[0], q[2])
                z.append((p[1], q[1]))
                base.append([part[0] for part in parts])
                for comp in range(2):
                    es[comp].append(east(parts[comp][1]))
                    ws[comp].append(west(parts[comp][2]))
            for comp in range(2):
                edge_e, edge_w = halo_column(1, comp, bi, r0), halo_column(0, comp, bi, r0)
                for bj in range(nbj):
                    right = es[comp][bj + 1] if bj < nbj - 1 else edge_e
                    left = ws[comp][bj - 1] if bj > 0 else edge_w
                    e = jnp.where(lane_s == BS - 1, right, es[comp][bj])
                    w = jnp.where(lane_s == 0, left, ws[comp][bj])
                    image = CO[2, bj, here, :] * z[bj][comp] - CO[3, bj, here, :] * (base[bj][comp] + e + w)
                    old = V[step, comp, bj, here, :]
                    new = image - old
                    if not last:
                        V[step + 1, comp, bj, here, :] = new
                        Z0[comp, bi * nbj + bj, pl.ds(PAD + r0, ROWS_S), :] = new * CO[0, bj, here, :]
                    for i in range(step + 1):
                        earlier = old if i == step else V[i, comp, bj, here, :]
                        acc[i] = acc[i] + fold(new * earlier)
                    acc[step + 1] = acc[step + 1] + fold(new * new)
            return tuple(acc)

        put_products(step + 1, lax.fori_loop(0, rows // ROWS_S, body, (zero8,) * (step + 2)))

    for step in range(STEPS):
        sweep(step)
        pending.append(send_halo(step, range(len(DIRS))))
        take_halo(step, pending[-1], True)
        operator(step)

    def spread(src, buffer, count, send, recv, along_row):
        moved = [
            pltpu.make_async_remote_copy(
                src_ref=src,
                dst_ref=buffer.at[o - 1],
                send_sem=send.at[o - 1],
                recv_sem=recv.at[o - 1],
                device_id=device(o, 0) if along_row else device(0, o),
                device_id_type=MESH,
            )
            for o in range(1, count)
        ]
        for copy in moved:
            copy.start()
        for copy in moved:
            copy.wait_recv()
        pending.append(moved)
        total = src[...]
        for o in range(1, count):
            total = total + buffer[o - 1]
        return total

    GX[...] = spread(GB, R1, n_row, s1, r1, True)
    products = jnp.sum(spread(GX, R2, n_col, s2, r2, False), axis=1, keepdims=True)
    weights = scalars([products[n : n + 1] for n in range(len(PAIRS))])

    for comp in range(2):
        for bj in range(nbj):
            total = None
            for step in range(STEPS):
                term = weights[step] * D[step, comp, bj, PAD : PAD + rows, :]
                total = term if total is None else total + term
            out_ref[comp, :, bj * BS : (bj + 1) * BS] = total
    for moved in pending:
        for copy in moved:
            copy.wait_send()


def solution(mesh):
    n_chip, n_row, n_grp = mesh.shape["chip"], mesh.shape["row"], mesh.shape["grp"]

    def shards(old_velocity, surface_stress, mass_term, ocean_drag, strength, ice_mask, ocean_mask, ice_blocks):
        _, rows, cols = old_velocity.shape
        nbi, nbj = rows // BS, cols // BS
        vmem = pl.BlockSpec(memory_space=pltpu.VMEM)
        f32 = jnp.float32
        n_col = n_chip * n_grp
        dma = pltpu.SemaphoreType.DMA
        return pl.pallas_call(
            functools.partial(kernel, (n_chip, n_row, n_grp, rows, cols)),
            out_shape=jax.ShapeDtypeStruct(old_velocity.shape, f32),
            in_specs=[vmem] * 7 + [pl.BlockSpec(memory_space=pltpu.SMEM)],
            out_specs=vmem,
            scratch_shapes=[
                pltpu.VMEM((STEPS + 1, 2, nbj, rows + 2 * PAD, BS), f32),
                pltpu.VMEM((STEPS, 2, nbj, rows, BS), f32),
                pltpu.VMEM((2, nbi * nbj, BS + 2 * PAD, BS), f32),
                pltpu.VMEM((2, nbi * nbj, BS + 2 * PAD, BS), f32),
                pltpu.VMEM((4, nbj, rows, BS), f32),
                pltpu.VMEM((STEPS + 1, 2, 8, BS), f32),
                pltpu.VMEM((STEPS + 1, 6, 8, BS), f32),
                pltpu.VMEM((2, 8, BS), f32),
                pltpu.VMEM((COUNT, BS), f32),
                pltpu.VMEM((COUNT, BS), f32),
                pltpu.VMEM((n_row - 1, COUNT, BS), f32),
                pltpu.VMEM((n_col - 1, COUNT, BS), f32),
                dma((STEPS + 1, len(DIRS))),
                dma((STEPS + 1, len(DIRS))),
                dma((n_row - 1,)),
                dma((n_row - 1,)),
                dma((n_col - 1,)),
                dma((n_col - 1,)),
            ],
            compiler_params=pltpu.CompilerParams(
                collective_id=0, has_side_effects=True, vmem_limit_bytes=40 * 1024 * 1024
            ),
        )(old_velocity, surface_stress, mass_term, ocean_drag, strength, ice_mask, ocean_mask, ice_blocks)

    return jax.shard_map(
        shards,
        mesh=mesh,
        in_specs=(
            P(None, "row", ("chip", "grp")),
            P(None, "row", ("chip", "grp")),
            P("row", ("chip", "grp")),
            P("row", ("chip", "grp")),
            P("row", ("chip", "grp")),
            P("row", ("chip", "grp")),
            P("row", ("chip", "grp")),
            P(("chip", "grp"), None),
        ),
        out_specs=P(None, "row", ("chip", "grp")),
        check_vma=False,
    )
```

```python
import functools

import jax
import jax.numpy as jnp
from jax import lax
from jax.experimental import pallas as pl
from jax.experimental.pallas import tpu as pltpu
from jax.sharding import PartitionSpec as P

MESH = pl.DeviceIdType.MESH
BS = 128
DMIN_SQ = 0.25
STEPS = 4
DEPTH = 16
PAD = 8
ROWS = 16
PACKED = BS // DEPTH
FIELDS = 6
DIAG = 4
DIRS = ((-1, 0), (1, 0), (0, 1), (1, 1), (-1, 1), (0, -1), (1, -1), (-1, -1))
PAIRS = [(i, j) for j in range(STEPS + 1) for i in range(j + 1)]
INDEX = {pair: n for n, pair in enumerate(PAIRS)}
COUNT = 16


def neighbour_sum(p, p_n, p_s, q, q_n, q_s):
    tq = q_s - q_n
    tp = p_s - p_n
    q5 = 5.0 * q
    return (5.0 * (p_n + p_s), p + tq, p - tq), (q_n + q_s, q5 + tp, q5 - tp)


def scalars(gram):
    n = STEPS + 1

    def g(i, j):
        return gram[INDEX[(min(i, j), max(i, j))]]

    def dot(x, y):
        total = None
        for j in range(n):
            if y[j] is None:
                continue
            inner = None
            for i in range(n):
                if x[i] is None:
                    continue
                term = x[i] * g(i, j)
                inner = term if inner is None else inner + term
            term = inner * y[j]
            total = term if total is None else total + term
        return total

    def shift(x):
        return [None] + x[: n - 1]

    def add(x, y):
        return [b if a is None else a if b is None else a + b for a, b in zip(x, y)]

    def cycle(r):
        w1 = add(r, shift(r))
        w2 = shift(w1)
        b1, b2 = dot(r, w1), dot(r, w2)
        g11, g12, g22 = dot(w1, w1), dot(w1, w2), dot(w2, w2)
        det = g11 * g22 - g12 * g12
        good = det > 0.0
        inv = 1.0 / jnp.where(good, det, 1.0)
        single = jnp.where(g11 > 0.0, b1 / jnp.where(g11 > 0.0, g11, 1.0), 0.0)
        a = jnp.where(good, (b1 * g22 - b2 * g12) * inv, single)
        b = jnp.where(good, (g11 * b2 - g12 * b1) * inv, 0.0)
        return a, b

    one = jnp.ones_like(gram[0])
    a0, b0 = cycle([one, None, None, None, None])
    c = [1.0 - a0, -(a0 + b0), -b0]
    a1, b1 = cycle(c + [None, None])
    return (
        a0 + a1 * c[0],
        b0 + a1 * c[1] + b1 * c[0],
        a1 * c[2] + b1 * c[1],
        b1 * c[2],
    )


def kernel(
    sizes,
    vel_hbm,
    stress_hbm,
    mass_hbm,
    drag_hbm,
    strength_hbm,
    ice_hbm,
    ocean_hbm,
    listed_ref,
    out_ref,
    vel_ref,
    stress_ref,
    mass_ref,
    drag_ref,
    strength_ref,
    ice_ref,
    ocean_ref,
    X,
    D,
    V,
    Z0,
    Z1,
    CO,
    PB,
    PR,
    CB,
    CR,
    GB,
    GX,
    R1,
    R2,
    load_sem,
    send_sem,
    recv_sem,
    s1,
    r1,
    s2,
    r2,
):
    n_chip, n_row, n_grp, rows, cols = sizes
    n_col = n_chip * n_grp
    nbi, nbj = rows // BS, cols // BS
    nl = nbj + 1
    group = rows // PACKED
    chunks = (rows + 2 * DEPTH) // ROWS
    per_block = BS // ROWS
    chip = lax.axis_index("chip")
    row = lax.axis_index("row")
    grp = lax.axis_index("grp")
    col = chip * n_grp + grp

    loads = [
        pltpu.make_async_copy(src, dst, load_sem.at[n])
        for n, (src, dst) in enumerate(
            (
                (vel_hbm, vel_ref),
                (mass_hbm, mass_ref),
                (ocean_hbm, ocean_ref),
                (stress_hbm, stress_ref),
                (drag_hbm, drag_ref),
                (strength_hbm, strength_ref),
                (ice_hbm, ice_ref),
            )
        )
    ]
    for load in loads:
        load.start()

    def device(dr, dc):
        r = lax.rem(row + (dr + n_row), n_row)
        c = lax.rem(col + (dc + n_col), n_col)
        return (lax.div(c, n_grp), r, lax.rem(c, n_grp))

    partners = list(DIRS)
    for o in range(2, n_row - 1):
        partners.append((o, 0))
    for o in range(2, n_col - 1):
        partners.append((0, o))
    barrier = pltpu.get_barrier_semaphore()
    for dr, dc in partners:
        pl.semaphore_signal(barrier, inc=1, device_id=device(dr, dc), device_id_type=MESH)

    has_n = row > 0
    has_s = row < n_row - 1
    has_w = col > 0
    has_e = col < n_col - 1

    def exists(dr, dc):
        found = None
        for offset, low, high in ((dr, has_n, has_s), (dc, has_w, has_e)):
            if offset:
                flag = low if offset < 0 else high
                found = flag if found is None else jnp.logical_and(found, flag)
        return found

    lane = lax.broadcasted_iota(jnp.int32, (ROWS, BS), 1)
    lane_g = lax.broadcasted_iota(jnp.int32, (group, BS), 1)
    first_lane, last_lane = lane == 0, lane == BS - 1

    def east(x):
        return pltpu.roll(x, BS - 1, 1)

    def west(x):
        return pltpu.roll(x, 1, 1)

    def turn(x, amount):
        amount = amount % BS
        return x if amount == 0 else pltpu.roll(x, amount, 1)

    def filling(field):
        return 1.0 if field == DIAG else 0.0

    zero8 = jnp.zeros((PAD, BS), jnp.float32)
    edges = [0, PAD + DEPTH]
    for b in range(nbi):
        edges.append(edges[-1] + PAD + BS)
    edges.append(edges[-1] + PAD + DEPTH)
    for j in range(nl):
        for comp in range(2):
            for at in edges:
                Z0[comp, j, at : at + PAD, :] = zero8
                Z1[comp, j, at : at + PAD, :] = zero8
            for at in (0, PAD + rows + 2 * DEPTH):
                X[comp, j, at : at + PAD, :] = zero8
                for step in range(STEPS):
                    D[step, comp, j, at : at + PAD, :] = zero8

    live = []
    for b in range(nbi * nbj):
        wanted = row * (nbi * nbj) + b
        flag = jnp.float32(0.0)
        for n in range(listed_ref.shape[1]):
            flag = jnp.maximum(flag, jnp.where(listed_ref[0, n] == wanted, 1.0, 0.0))
        live.append(flag)

    for load in loads:
        load.wait()

    def local(t, carry):
        bi = lax.div(t, per_block)
        start = pl.multiple_of(t * ROWS, ROWS)
        here = pl.ds(start, ROWS)
        there = pl.ds(pl.multiple_of(PAD + DEPTH + start, PAD), ROWS)
        for j in range(nbj):
            lanes = slice(j * BS, (j + 1) * BS)
            flag = live[j]
            for b in range(1, nbi):
                flag = jnp.where(bi == b, live[b * nbj + j], flag)
            ocean = ocean_ref[here, lanes].astype(jnp.float32)
            ice = ice_ref[here, lanes].astype(jnp.float32)
            mass = mass_ref[here, lanes]
            scaled = flag * ocean
            for comp in range(2):
                vel = vel_ref[comp, here, lanes]
                X[comp, j, there, :] = vel
                X[2 + comp, j, there, :] = scaled * (stress_ref[comp, here, lanes] + mass * vel)
            X[DIAG, j, there, :] = ocean * (mass + drag_ref[here, lanes]) + (1.0 - ocean)
            X[5, j, there, :] = scaled * ice * strength_ref[here, lanes]
        return carry

    lax.fori_loop(0, rows // ROWS, local, 0)

    base = PAD + DEPTH
    for side, j in ((0, nbj - 1), (1, 0)):
        shift = DEPTH if side == 0 else 0

        def pack(field, carry, side=side, j=j, shift=shift):
            packed = jnp.zeros((group, BS), jnp.float32)
            for g in range(PACKED):
                x = X[field, j, base + g * group : base + (g + 1) * group, :]
                mine = jnp.logical_and(lane_g >= g * DEPTH, lane_g < (g + 1) * DEPTH)
                packed = jnp.where(mine, turn(x, g * DEPTH + shift), packed)
            PB[side, field] = packed
            return carry

        lax.fori_loop(0, FIELDS, pack, 0)
        for low in range(2):
            first = base + (rows - DEPTH if low else 0)
            packed = jnp.zeros((DEPTH, BS), jnp.float32)
            for field in range(FIELDS):
                x = X[field, j, first : first + DEPTH, :]
                mine = jnp.logical_and(lane >= field * DEPTH, lane < (field + 1) * DEPTH)
                packed = jnp.where(mine, turn(x, field * DEPTH + shift), packed)
            CB[2 * side + low] = packed

    moved = []
    for d, (dr, dc) in enumerate(DIRS):
        if dc == 0:
            first, there = (base, base + rows) if dr < 0 else (base + rows - DEPTH, PAD)
            src = X.at[:, pl.ds(0, nbj), pl.ds(first, DEPTH), :]
            dst = X.at[:, pl.ds(0, nbj), pl.ds(there, DEPTH), :]
        elif dr == 0:
            side = 0 if dc > 0 else 1
            src, dst = PB.at[side], PR.at[side]
        else:
            n = (0 if dc > 0 else 2) + (1 if dr > 0 else 0)
            src, dst = CB.at[n], CR.at[n]
        moved.append(
            pltpu.make_async_remote_copy(
                src_ref=src,
                dst_ref=dst,
                send_sem=send_sem.at[d],
                recv_sem=recv_sem.at[d],
                device_id=device(dr, dc),
                device_id_type=MESH,
            )
        )
    pl.semaphore_wait(barrier, len(partners))
    for d in (2, 5, 0, 1, 3, 4, 6, 7):
        pl.when(exists(*DIRS[d]))(moved[d].start)
    for d in (0, 1, 2, 5, 3, 4, 6, 7):
        dr, dc = DIRS[d]
        pl.when(exists(-dr, -dc))(moved[d].wait_recv)

    for field in range(FIELDS):
        fill = filling(field)
        for j in range(nbj):
            for at, flag in ((PAD, has_n), (base + rows, has_s)):
                X[field, j, at : at + DEPTH, :] = jnp.where(flag, X[field, j, at : at + DEPTH, :], fill)
        for low, at, flag in ((1, PAD, has_n), (0, base + rows, has_s)):
            from_w = turn(CR[low], -(field * DEPTH + DEPTH))
            from_e = turn(CR[2 + low], -(field * DEPTH))
            is_w = jnp.logical_and(lane >= BS - DEPTH, jnp.logical_and(flag, has_w))
            is_e = jnp.logical_and(lane < DEPTH, jnp.logical_and(flag, has_e))
            X[field, nbj, at : at + DEPTH, :] = jnp.where(is_e, from_e, jnp.where(is_w, from_w, fill))

    def unpack(field, carry):
        fill = jnp.where(field == DIAG, 1.0, 0.0)
        w, e = PR[0, field], PR[1, field]
        is_w = jnp.logical_and(lane_g >= BS - DEPTH, has_w)
        is_e = jnp.logical_and(lane_g < DEPTH, has_e)
        for g in range(PACKED):
            from_w = turn(w, -(g * DEPTH + DEPTH))
            from_e = turn(e, -(g * DEPTH))
            X[field, nbj, base + g * group : base + (g + 1) * group, :] = jnp.where(
                is_e, from_e, jnp.where(is_w, from_w, fill)
            )
        return carry

    lax.fori_loop(0, FIELDS, unpack, 0)

    def fold(x):
        total = x[0:8]
        for n in range(1, ROWS // 8):
            total = total + x[8 * n : 8 * n + 8]
        return total

    def sweep_row(t):
        per = per_block * nbi
        shift = 1 + lax.div(t + (per - 1), per)
        for b in range(1, nbi):
            shift = shift + lax.div(t + (per - 1 - b * per_block), per)
        return pl.multiple_of(t * ROWS + PAD * shift, PAD)

    def neighbours(ref, index, j, first):
        return [ref[index + (j, pl.ds(first + d, ROWS))] for d in (-1, 0, 1)]

    def across(es, ws, j, ring):
        if ring:
            right, left = es[(j + 1) % nl], ws[(j - 1) % nl]
        else:
            right, left = 0.0, 0.0
        return jnp.where(last_lane, right, es[j]), jnp.where(first_lane, left, ws[j])

    def setup(t, acc, own):
        start = pl.multiple_of(t * ROWS, ROWS)
        here = pl.ds(start, ROWS)
        inside = pl.ds(pl.multiple_of(PAD + start, PAD), ROWS)
        at = sweep_row(t)
        us = [neighbours(X, (0,), j, PAD + start) for j in range(nl)]
        vs = [neighbours(X, (1,), j, PAD + start) for j in range(nl)]
        eu, wu = [east(x[1]) for x in us], [west(x[1]) for x in us]
        ev, wv = [east(x[1]) for x in vs], [west(x[1]) for x in vs]
        for j in range(nl):
            u_e, u_w = across(eu, wu, j, True)
            v_e, v_w = across(ev, wv, j, True)
            e11 = 0.5 * (us[j][2] - us[j][0])
            e22 = 0.5 * (v_e - v_w)
            e12 = 0.25 * (u_e - u_w + vs[j][2] - vs[j][0])
            deform = 1.25 * (e11 * e11 + e22 * e22) + e12 * e12 + 1.5 * e11 * e22
            zeta = X[5, j, inside, :] / (2.0 * jnp.sqrt(deform + DMIN_SQ))
            total = X[DIAG, j, inside, :] + 3.0 * zeta
            inv = 1.0 / total
            CO[0, j, here, :] = inv
            CO[1, j, here, :] = 0.2 * zeta * inv
            CO[2, j, here, :] = total
            CO[3, j, here, :] = 0.25 * zeta
            for comp in range(2):
                rhs = X[2 + comp, j, inside, :]
                V[0, comp, j, here, :] = rhs
                Z0[comp, j, pl.ds(at, ROWS), :] = rhs * inv
                if own and j < nbj:
                    acc = acc + fold(rhs * rhs)
        return acc

    def put_products(step, values):
        for i, value in enumerate(values):
            n = INDEX[(i, step)]
            GB[n : n + 1, :] = jnp.sum(value, axis=0, keepdims=True)

    GB[COUNT - 1 : COUNT, :] = jnp.zeros((1, BS), jnp.float32)
    for t in (0, chunks - 1):
        setup(t, None, False)
    put_products(0, [lax.fori_loop(1, chunks - 1, lambda t, acc: setup(t, acc, True), zero8)])

    def block_sums(Z, j, at):
        p, q = neighbours(Z, (0,), j, at), neighbours(Z, (1,), j, at)
        sums = []
        for middle, ye, yw in neighbour_sum(p[1], p[0], p[2], q[1], q[0], q[2]):
            sums.append(
                middle + jnp.where(last_lane, 0.0, east(ye)) + jnp.where(first_lane, 0.0, west(yw))
            )
        return (p[1], q[1]), sums

    def sweep(step):
        def first(t, carry):
            at = sweep_row(t)
            here = pl.ds(pl.multiple_of(t * ROWS, ROWS), ROWS)
            for j in range(nl):
                z, sums = block_sums(Z0, j, at)
                k = CO[1, j, here, :]
                for comp in range(2):
                    Z1[comp, j, pl.ds(at, ROWS), :] = z[comp] + k * sums[comp]
            return carry

        def second(t, carry):
            at = sweep_row(t)
            start = pl.multiple_of(t * ROWS, ROWS)
            for j in range(nl):
                z, sums = block_sums(Z1, j, at)
                k = CO[1, j, pl.ds(start, ROWS), :]
                for comp in range(2):
                    z0 = Z0[comp, j, pl.ds(at, ROWS), :]
                    D[step, comp, j, pl.ds(pl.multiple_of(PAD + start, PAD), ROWS), :] = (
                        0.2 * z[comp] + 0.8 * z0 + k * sums[comp]
                    )
            return carry

        lax.fori_loop(0, chunks, first, 0)
        lax.fori_loop(0, chunks, second, 0)

    def operator(step):
        last = step == STEPS - 1

        def body(t, acc, own):
            acc = list(acc)
            at = sweep_row(t)
            start = pl.multiple_of(t * ROWS, ROWS)
            here = pl.ds(start, ROWS)
            z, middle, es, ws = [], [], [[], []], [[], []]
            for j in range(nl):
                p = neighbours(D, (step, 0), j, PAD + start)
                q = neighbours(D, (step, 1), j, PAD + start)
                parts = neighbour_sum(p[1], p[0], p[2], q[1], q[0], q[2])
                z.append((p[1], q[1]))
                middle.append([part[0] for part in parts])
                for comp in range(2):
                    es[comp].append(east(parts[comp][1]))
                    ws[comp].append(west(parts[comp][2]))
            for comp in range(2):
                for j in range(nbj if last else nl):
                    e, w = across(es[comp], ws[comp], j, True)
                    image = CO[2, j, here, :] * z[j][comp] - CO[3, j, here, :] * (middle[j][comp] + e + w)
                    old = V[step, comp, j, here, :]
                    new = image - old
                    if not last:
                        V[step + 1, comp, j, here, :] = new
                        Z0[comp, j, pl.ds(at, ROWS), :] = new * CO[0, j, here, :]
                    if own and j < nbj:
                        for i in range(step + 1):
                            earlier = old if i == step else V[i, comp, j, here, :]
                            acc[i] = acc[i] + fold(new * earlier)
                        acc[step + 1] = acc[step + 1] + fold(new * new)
            return tuple(acc)

        if not last:
            for t in (0, chunks - 1):
                body(t, (), False)
        start = (zero8,) * (step + 2)
        put_products(step + 1, lax.fori_loop(1, chunks - 1, lambda t, acc: body(t, acc, True), start))

    for step in range(STEPS):
        sweep(step)
        operator(step)

    pending = []

    def spread(src, buffer, count, send, recv, along_row):
        out = [
            pltpu.make_async_remote_copy(
                src_ref=src,
                dst_ref=buffer.at[o - 1],
                send_sem=send.at[o - 1],
                recv_sem=recv.at[o - 1],
                device_id=device(o, 0) if along_row else device(0, o),
                device_id_type=MESH,
            )
            for o in range(1, count)
        ]
        for copy in out:
            copy.start()
        for copy in out:
            copy.wait_recv()
        pending.extend(out)
        total = src[...]
        for o in range(1, count):
            total = total + buffer[o - 1]
        return total

    GX[...] = spread(GB, R1, n_row, s1, r1, True)
    products = jnp.sum(spread(GX, R2, n_col, s2, r2, False), axis=1, keepdims=True)
    weights = scalars([products[n : n + 1] for n in range(len(PAIRS))])

    for comp in range(2):
        for j in range(nbj):
            total = None
            for step in range(STEPS):
                term = weights[step] * D[step, comp, j, base : base + rows, :]
                total = term if total is None else total + term
            out_ref[comp, :, j * BS : (j + 1) * BS] = total
    for d, (dr, dc) in enumerate(DIRS):
        pl.when(exists(dr, dc))(moved[d].wait_send)
    for copy in pending:
        copy.wait_send()


def solution(mesh):
    n_chip, n_row, n_grp = mesh.shape["chip"], mesh.shape["row"], mesh.shape["grp"]

    def shards(old_velocity, surface_stress, mass_term, ocean_drag, strength, ice_mask, ocean_mask, ice_blocks):
        _, rows, cols = old_velocity.shape
        nbi, nbj = rows // BS, cols // BS
        nl, long = nbj + 1, rows + 2 * DEPTH
        vmem = pl.BlockSpec(memory_space=pltpu.VMEM)
        f32 = jnp.float32
        n_col = n_chip * n_grp
        dma = pltpu.SemaphoreType.DMA
        return pl.pallas_call(
            functools.partial(kernel, (n_chip, n_row, n_grp, rows, cols)),
            out_shape=jax.ShapeDtypeStruct(old_velocity.shape, f32),
            in_specs=[pl.BlockSpec(memory_space=pl.ANY)] * 7 + [pl.BlockSpec(memory_space=pltpu.SMEM)],
            out_specs=vmem,
            scratch_shapes=[
                pltpu.VMEM(old_velocity.shape, f32),
                pltpu.VMEM(old_velocity.shape, f32),
                pltpu.VMEM((rows, cols), f32),
                pltpu.VMEM((rows, cols), f32),
                pltpu.VMEM((rows, cols), f32),
                pltpu.VMEM((rows, cols), jnp.int32),
                pltpu.VMEM((rows, cols), jnp.int32),
                pltpu.VMEM((FIELDS, nl, long + 2 * PAD, BS), f32),
                pltpu.VMEM((STEPS, 2, nl, long + 2 * PAD, BS), f32),
                pltpu.VMEM((STEPS, 2, nl, long, BS), f32),
                pltpu.VMEM((2, nl, long + (nbi + 3) * PAD, BS), f32),
                pltpu.VMEM((2, nl, long + (nbi + 3) * PAD, BS), f32),
                pltpu.VMEM((4, nl, long, BS), f32),
                pltpu.VMEM((2, FIELDS, rows // PACKED, BS), f32),
                pltpu.VMEM((2, FIELDS, rows // PACKED, BS), f32),
                pltpu.VMEM((4, DEPTH, BS), f32),
                pltpu.VMEM((4, DEPTH, BS), f32),
                pltpu.VMEM((COUNT, BS), f32),
                pltpu.VMEM((COUNT, BS), f32),
                pltpu.VMEM((n_row - 1, COUNT, BS), f32),
                pltpu.VMEM((n_col - 1, COUNT, BS), f32),
                dma((7,)),
                dma((len(DIRS),)),
                dma((len(DIRS),)),
                dma((n_row - 1,)),
                dma((n_row - 1,)),
                dma((n_col - 1,)),
                dma((n_col - 1,)),
            ],
            compiler_params=pltpu.CompilerParams(
                collective_id=0, has_side_effects=True, vmem_limit_bytes=60 * 1024 * 1024
            ),
        )(old_velocity, surface_stress, mass_term, ocean_drag, strength, ice_mask, ocean_mask, ice_blocks)

    return jax.shard_map(
        shards,
        mesh=mesh,
        in_specs=(
            P(None, "row", ("chip", "grp")),
            P(None, "row", ("chip", "grp")),
            P("row", ("chip", "grp")),
            P("row", ("chip", "grp")),
            P("row", ("chip", "grp")),
            P("row", ("chip", "grp")),
            P("row", ("chip", "grp")),
            P(("chip", "grp"), None),
        ),
        out_specs=P(None, "row", ("chip", "grp")),
        check_vma=False,
    )
```

```python
import functools

import jax
import jax.numpy as jnp
from jax import lax
from jax.experimental import pallas as pl
from jax.experimental.pallas import tpu as pltpu
from jax.sharding import PartitionSpec as P

MESH = pl.DeviceIdType.MESH
BS = 128
DMIN_SQ = 0.25
STEPS = 4
DEPTH = 16
PAD = 8
ROWS = 16
PACKED = BS // DEPTH
FIELDS = 6
DIAG = 4
DIRS = ((-1, 0), (1, 0), (0, 1), (1, 1), (-1, 1), (0, -1), (1, -1), (-1, -1))
PAIRS = [(i, j) for j in range(STEPS + 1) for i in range(j + 1)]
INDEX = {pair: n for n, pair in enumerate(PAIRS)}
COUNT = 16
UNROLL_LOCAL = 16
UNROLL_SETUP = 16
UNROLL_SWEEP = 18
UNROLL_OPERATOR = 16


def neighbour_sum(p, p_n, p_s, q, q_n, q_s):
    tq = q_s - q_n
    tp = p_s - p_n
    q5 = 5.0 * q
    return (5.0 * (p_n + p_s), p + tq, p - tq), (q_n + q_s, q5 + tp, q5 - tp)


def aligned(index, multiple):
    return index if isinstance(index, int) else pl.multiple_of(index, multiple)


def chunked(low, high, unroll, body, carry):
    count = high - low
    if count <= unroll:
        for t in range(low, high):
            carry = body(t, carry)
        return carry

    def several(n, carry):
        for i in range(unroll):
            carry = body(low + n * unroll + i, carry)
        return carry

    carry = lax.fori_loop(0, count // unroll, several, carry)
    for t in range(low + count // unroll * unroll, high):
        carry = body(t, carry)
    return carry


def scalars(gram):
    n = STEPS + 1

    def g(i, j):
        return gram[INDEX[(min(i, j), max(i, j))]]

    def dot(x, y):
        total = None
        for j in range(n):
            if y[j] is None:
                continue
            inner = None
            for i in range(n):
                if x[i] is None:
                    continue
                term = x[i] * g(i, j)
                inner = term if inner is None else inner + term
            term = inner * y[j]
            total = term if total is None else total + term
        return total

    def shift(x):
        return [None] + x[: n - 1]

    def add(x, y):
        return [b if a is None else a if b is None else a + b for a, b in zip(x, y)]

    def cycle(r):
        w1 = add(r, shift(r))
        w2 = shift(w1)
        b1, b2 = dot(r, w1), dot(r, w2)
        g11, g12, g22 = dot(w1, w1), dot(w1, w2), dot(w2, w2)
        det = g11 * g22 - g12 * g12
        good = det > 0.0
        inv = 1.0 / jnp.where(good, det, 1.0)
        single = jnp.where(g11 > 0.0, b1 / jnp.where(g11 > 0.0, g11, 1.0), 0.0)
        a = jnp.where(good, (b1 * g22 - b2 * g12) * inv, single)
        b = jnp.where(good, (g11 * b2 - g12 * b1) * inv, 0.0)
        return a, b

    one = jnp.ones_like(gram[0])
    a0, b0 = cycle([one, None, None, None, None])
    c = [1.0 - a0, -(a0 + b0), -b0]
    a1, b1 = cycle(c + [None, None])
    return (
        a0 + a1 * c[0],
        b0 + a1 * c[1] + b1 * c[0],
        a1 * c[2] + b1 * c[1],
        b1 * c[2],
    )


def kernel(
    sizes,
    vel_hbm,
    stress_hbm,
    mass_hbm,
    drag_hbm,
    strength_hbm,
    ice_hbm,
    ocean_hbm,
    listed_ref,
    out_ref,
    vel_ref,
    stress_ref,
    mass_ref,
    drag_ref,
    strength_ref,
    ice_ref,
    ocean_ref,
    X,
    D,
    V,
    Z0,
    Z1,
    CO,
    PB,
    PR,
    CB,
    CR,
    GB,
    GX,
    R1,
    R2,
    load_sem,
    send_sem,
    recv_sem,
    s1,
    r1,
    s2,
    r2,
):
    n_chip, n_row, n_grp, rows, cols = sizes
    n_col = n_chip * n_grp
    nbi, nbj = rows // BS, cols // BS
    nl = nbj + 1
    group = rows // PACKED
    chunks = (rows + 2 * DEPTH) // ROWS
    per_block = BS // ROWS
    chip = lax.axis_index("chip")
    row = lax.axis_index("row")
    grp = lax.axis_index("grp")
    col = chip * n_grp + grp

    loads = [
        pltpu.make_async_copy(src, dst, load_sem.at[n])
        for n, (src, dst) in enumerate(
            (
                (vel_hbm, vel_ref),
                (mass_hbm, mass_ref),
                (ocean_hbm, ocean_ref),
                (stress_hbm, stress_ref),
                (drag_hbm, drag_ref),
                (strength_hbm, strength_ref),
                (ice_hbm, ice_ref),
            )
        )
    ]
    for load in loads:
        load.start()

    def device(dr, dc):
        r = lax.rem(row + (dr + n_row), n_row)
        c = lax.rem(col + (dc + n_col), n_col)
        return (lax.div(c, n_grp), r, lax.rem(c, n_grp))

    partners = list(DIRS)
    for o in range(2, n_row - 1):
        partners.append((o, 0))
    for o in range(2, n_col - 1):
        partners.append((0, o))
    barrier = pltpu.get_barrier_semaphore()
    for dr, dc in partners:
        pl.semaphore_signal(barrier, inc=1, device_id=device(dr, dc), device_id_type=MESH)

    has_n = row > 0
    has_s = row < n_row - 1
    has_w = col > 0
    has_e = col < n_col - 1

    def exists(dr, dc):
        found = None
        for offset, low, high in ((dr, has_n, has_s), (dc, has_w, has_e)):
            if offset:
                flag = low if offset < 0 else high
                found = flag if found is None else jnp.logical_and(found, flag)
        return found

    lane = lax.broadcasted_iota(jnp.int32, (ROWS, BS), 1)
    lane_g = lax.broadcasted_iota(jnp.int32, (group, BS), 1)
    first_lane, last_lane = lane == 0, lane == BS - 1

    def east(x):
        return pltpu.roll(x, BS - 1, 1)

    def west(x):
        return pltpu.roll(x, 1, 1)

    def turn(x, amount):
        amount = amount % BS
        return x if amount == 0 else pltpu.roll(x, amount, 1)

    def filling(field):
        return 1.0 if field == DIAG else 0.0

    zero8 = jnp.zeros((PAD, BS), jnp.float32)
    edges = [0, PAD + DEPTH]
    for b in range(nbi):
        edges.append(edges[-1] + PAD + BS)
    edges.append(edges[-1] + PAD + DEPTH)
    for j in range(nl):
        for comp in range(2):
            for at in edges:
                Z0[comp, j, at : at + PAD, :] = zero8
                Z1[comp, j, at : at + PAD, :] = zero8
            for at in (0, PAD + rows + 2 * DEPTH):
                X[comp, j, at : at + PAD, :] = zero8
                for step in range(STEPS):
                    D[step, comp, j, at : at + PAD, :] = zero8

    live = []
    for b in range(nbi * nbj):
        wanted = row * (nbi * nbj) + b
        flag = jnp.float32(0.0)
        for n in range(listed_ref.shape[1]):
            flag = jnp.maximum(flag, jnp.where(listed_ref[0, n] == wanted, 1.0, 0.0))
        live.append(flag)

    for load in loads:
        load.wait()

    def local(t, carry):
        bi = t // per_block if isinstance(t, int) else lax.div(t, per_block)
        start = aligned(t * ROWS, ROWS)
        here = pl.ds(start, ROWS)
        there = pl.ds(aligned(PAD + DEPTH + start, PAD), ROWS)
        for j in range(nbj):
            lanes = slice(j * BS, (j + 1) * BS)
            flag = live[j]
            for b in range(1, nbi):
                flag = jnp.where(bi == b, live[b * nbj + j], flag)
            ocean = ocean_ref[here, lanes].astype(jnp.float32)
            ice = ice_ref[here, lanes].astype(jnp.float32)
            mass = mass_ref[here, lanes]
            scaled = flag * ocean
            for comp in range(2):
                vel = vel_ref[comp, here, lanes]
                X[comp, j, there, :] = vel
                X[2 + comp, j, there, :] = scaled * (stress_ref[comp, here, lanes] + mass * vel)
            X[DIAG, j, there, :] = ocean * (mass + drag_ref[here, lanes]) + (1.0 - ocean)
            X[5, j, there, :] = scaled * ice * strength_ref[here, lanes]
        return carry

    chunked(0, rows // ROWS, UNROLL_LOCAL, local, 0)

    base = PAD + DEPTH
    for side, j in ((0, nbj - 1), (1, 0)):
        shift = DEPTH if side == 0 else 0

        def pack(field, carry, side=side, j=j, shift=shift):
            packed = jnp.zeros((group, BS), jnp.float32)
            for g in range(PACKED):
                x = X[field, j, base + g * group : base + (g + 1) * group, :]
                mine = jnp.logical_and(lane_g >= g * DEPTH, lane_g < (g + 1) * DEPTH)
                packed = jnp.where(mine, turn(x, g * DEPTH + shift), packed)
            PB[side, field] = packed
            return carry

        lax.fori_loop(0, FIELDS, pack, 0)
        for low in range(2):
            first = base + (rows - DEPTH if low else 0)
            packed = jnp.zeros((DEPTH, BS), jnp.float32)
            for field in range(FIELDS):
                x = X[field, j, first : first + DEPTH, :]
                mine = jnp.logical_and(lane >= field * DEPTH, lane < (field + 1) * DEPTH)
                packed = jnp.where(mine, turn(x, field * DEPTH + shift), packed)
            CB[2 * side + low] = packed

    moved = []
    for d, (dr, dc) in enumerate(DIRS):
        if dc == 0:
            first, there = (base, base + rows) if dr < 0 else (base + rows - DEPTH, PAD)
            src = X.at[:, pl.ds(0, nbj), pl.ds(first, DEPTH), :]
            dst = X.at[:, pl.ds(0, nbj), pl.ds(there, DEPTH), :]
        elif dr == 0:
            side = 0 if dc > 0 else 1
            src, dst = PB.at[side], PR.at[side]
        else:
            n = (0 if dc > 0 else 2) + (1 if dr > 0 else 0)
            src, dst = CB.at[n], CR.at[n]
        moved.append(
            pltpu.make_async_remote_copy(
                src_ref=src,
                dst_ref=dst,
                send_sem=send_sem.at[d],
                recv_sem=recv_sem.at[d],
                device_id=device(dr, dc),
                device_id_type=MESH,
            )
        )
    pl.semaphore_wait(barrier, len(partners))
    for d in (2, 5, 0, 1, 3, 4, 6, 7):
        pl.when(exists(*DIRS[d]))(moved[d].start)
    for d in (0, 1, 2, 5, 3, 4, 6, 7):
        dr, dc = DIRS[d]
        pl.when(exists(-dr, -dc))(moved[d].wait_recv)

    for field in range(FIELDS):
        fill = filling(field)
        for j in range(nbj):
            for at, flag in ((PAD, has_n), (base + rows, has_s)):
                X[field, j, at : at + DEPTH, :] = jnp.where(flag, X[field, j, at : at + DEPTH, :], fill)
        for low, at, flag in ((1, PAD, has_n), (0, base + rows, has_s)):
            from_w = turn(CR[low], -(field * DEPTH + DEPTH))
            from_e = turn(CR[2 + low], -(field * DEPTH))
            is_w = jnp.logical_and(lane >= BS - DEPTH, jnp.logical_and(flag, has_w))
            is_e = jnp.logical_and(lane < DEPTH, jnp.logical_and(flag, has_e))
            X[field, nbj, at : at + DEPTH, :] = jnp.where(is_e, from_e, jnp.where(is_w, from_w, fill))

    def unpack(field, carry):
        fill = jnp.where(field == DIAG, 1.0, 0.0)
        w, e = PR[0, field], PR[1, field]
        is_w = jnp.logical_and(lane_g >= BS - DEPTH, has_w)
        is_e = jnp.logical_and(lane_g < DEPTH, has_e)
        for g in range(PACKED):
            from_w = turn(w, -(g * DEPTH + DEPTH))
            from_e = turn(e, -(g * DEPTH))
            X[field, nbj, base + g * group : base + (g + 1) * group, :] = jnp.where(
                is_e, from_e, jnp.where(is_w, from_w, fill)
            )
        return carry

    lax.fori_loop(0, FIELDS, unpack, 0)

    def fold(x):
        total = x[0:8]
        for n in range(1, ROWS // 8):
            total = total + x[8 * n : 8 * n + 8]
        return total

    def sweep_row(t):
        per = per_block * nbi
        if isinstance(t, int):
            return t * ROWS + PAD * (1 + sum((t + per - 1 - b * per_block) // per for b in range(nbi)))
        shift = 1
        for b in range(nbi):
            shift = shift + lax.div(t + (per - 1 - b * per_block), per)
        return aligned(t * ROWS + PAD * shift, PAD)

    def neighbours(ref, index, j, first):
        return [ref[index + (j, pl.ds(first + d, ROWS))] for d in (-1, 0, 1)]

    def across(es, ws, j, ring):
        if ring:
            right, left = es[(j + 1) % nl], ws[(j - 1) % nl]
        else:
            right, left = 0.0, 0.0
        return jnp.where(last_lane, right, es[j]), jnp.where(first_lane, left, ws[j])

    def setup(t, acc, own):
        start = aligned(t * ROWS, ROWS)
        here = pl.ds(start, ROWS)
        inside = pl.ds(aligned(PAD + start, PAD), ROWS)
        at = sweep_row(t)
        us = [neighbours(X, (0,), j, PAD + start) for j in range(nl)]
        vs = [neighbours(X, (1,), j, PAD + start) for j in range(nl)]
        eu, wu = [east(x[1]) for x in us], [west(x[1]) for x in us]
        ev, wv = [east(x[1]) for x in vs], [west(x[1]) for x in vs]
        for j in range(nl):
            u_e, u_w = across(eu, wu, j, True)
            v_e, v_w = across(ev, wv, j, True)
            e11 = 0.5 * (us[j][2] - us[j][0])
            e22 = 0.5 * (v_e - v_w)
            e12 = 0.25 * (u_e - u_w + vs[j][2] - vs[j][0])
            deform = 1.25 * (e11 * e11 + e22 * e22) + e12 * e12 + 1.5 * e11 * e22
            zeta = X[5, j, inside, :] / (2.0 * jnp.sqrt(deform + DMIN_SQ))
            total = X[DIAG, j, inside, :] + 3.0 * zeta
            inv = 1.0 / total
            CO[0, j, here, :] = inv
            CO[1, j, here, :] = 0.2 * zeta * inv
            CO[2, j, here, :] = total
            CO[3, j, here, :] = 0.25 * zeta
            for comp in range(2):
                rhs = X[2 + comp, j, inside, :]
                V[0, comp, j, here, :] = rhs
                Z0[comp, j, pl.ds(at, ROWS), :] = rhs * inv
                if own and j < nbj:
                    acc = acc + fold(rhs * rhs)
        return acc

    def put_products(step, values):
        for i, value in enumerate(values):
            n = INDEX[(i, step)]
            GB[n : n + 1, :] = jnp.sum(value, axis=0, keepdims=True)

    GB[COUNT - 1 : COUNT, :] = jnp.zeros((1, BS), jnp.float32)
    for t in (0, chunks - 1):
        setup(t, None, False)
    put_products(0, [chunked(1, chunks - 1, UNROLL_SETUP, lambda t, acc: setup(t, acc, True), zero8)])

    def block_sums(Z, j, at):
        p, q = neighbours(Z, (0,), j, at), neighbours(Z, (1,), j, at)
        sums = []
        for middle, ye, yw in neighbour_sum(p[1], p[0], p[2], q[1], q[0], q[2]):
            sums.append(
                middle + jnp.where(last_lane, 0.0, east(ye)) + jnp.where(first_lane, 0.0, west(yw))
            )
        return (p[1], q[1]), sums

    def sweep(step):
        def first(t, carry):
            at = sweep_row(t)
            here = pl.ds(aligned(t * ROWS, ROWS), ROWS)
            for j in range(nl):
                z, sums = block_sums(Z0, j, at)
                k = CO[1, j, here, :]
                for comp in range(2):
                    Z1[comp, j, pl.ds(at, ROWS), :] = z[comp] + k * sums[comp]
            return carry

        def second(t, carry):
            at = sweep_row(t)
            start = aligned(t * ROWS, ROWS)
            for j in range(nl):
                z, sums = block_sums(Z1, j, at)
                k = CO[1, j, pl.ds(start, ROWS), :]
                for comp in range(2):
                    z0 = Z0[comp, j, pl.ds(at, ROWS), :]
                    D[step, comp, j, pl.ds(aligned(PAD + start, PAD), ROWS), :] = (
                        0.2 * z[comp] + 0.8 * z0 + k * sums[comp]
                    )
            return carry

        chunked(0, chunks, UNROLL_SWEEP, first, 0)
        chunked(0, chunks, UNROLL_SWEEP, second, 0)

    def operator(step):
        last = step == STEPS - 1

        def body(t, acc, own):
            acc = list(acc)
            at = sweep_row(t)
            start = aligned(t * ROWS, ROWS)
            here = pl.ds(start, ROWS)
            z, middle, es, ws = [], [], [[], []], [[], []]
            for j in range(nl):
                p = neighbours(D, (step, 0), j, PAD + start)
                q = neighbours(D, (step, 1), j, PAD + start)
                parts = neighbour_sum(p[1], p[0], p[2], q[1], q[0], q[2])
                z.append((p[1], q[1]))
                middle.append([part[0] for part in parts])
                for comp in range(2):
                    es[comp].append(east(parts[comp][1]))
                    ws[comp].append(west(parts[comp][2]))
            for comp in range(2):
                for j in range(nbj if last else nl):
                    e, w = across(es[comp], ws[comp], j, True)
                    image = CO[2, j, here, :] * z[j][comp] - CO[3, j, here, :] * (middle[j][comp] + e + w)
                    old = V[step, comp, j, here, :]
                    new = image - old
                    if not last:
                        V[step + 1, comp, j, here, :] = new
                        Z0[comp, j, pl.ds(at, ROWS), :] = new * CO[0, j, here, :]
                    if own and j < nbj:
                        for i in range(step + 1):
                            earlier = old if i == step else V[i, comp, j, here, :]
                            acc[i] = acc[i] + fold(new * earlier)
                        acc[step + 1] = acc[step + 1] + fold(new * new)
            return tuple(acc)

        if not last:
            for t in (0, chunks - 1):
                body(t, (), False)
        start = (zero8,) * (step + 2)
        put_products(step + 1, chunked(1, chunks - 1, UNROLL_OPERATOR, lambda t, acc: body(t, acc, True), start))

    for step in range(STEPS):
        sweep(step)
        operator(step)

    pending = []

    def spread(src, buffer, count, send, recv, along_row):
        out = [
            pltpu.make_async_remote_copy(
                src_ref=src,
                dst_ref=buffer.at[o - 1],
                send_sem=send.at[o - 1],
                recv_sem=recv.at[o - 1],
                device_id=device(o, 0) if along_row else device(0, o),
                device_id_type=MESH,
            )
            for o in range(1, count)
        ]
        for copy in out:
            copy.start()
        for copy in out:
            copy.wait_recv()
        pending.extend(out)
        total = src[...]
        for o in range(1, count):
            total = total + buffer[o - 1]
        return total

    GX[...] = spread(GB, R1, n_row, s1, r1, True)
    products = jnp.sum(spread(GX, R2, n_col, s2, r2, False), axis=1, keepdims=True)
    weights = scalars([products[n : n + 1] for n in range(len(PAIRS))])

    for comp in range(2):
        for j in range(nbj):
            total = None
            for step in range(STEPS):
                term = weights[step] * D[step, comp, j, base : base + rows, :]
                total = term if total is None else total + term
            out_ref[comp, :, j * BS : (j + 1) * BS] = total
    for d, (dr, dc) in enumerate(DIRS):
        pl.when(exists(dr, dc))(moved[d].wait_send)
    for copy in pending:
        copy.wait_send()


def solution(mesh):
    n_chip, n_row, n_grp = mesh.shape["chip"], mesh.shape["row"], mesh.shape["grp"]

    def shards(old_velocity, surface_stress, mass_term, ocean_drag, strength, ice_mask, ocean_mask, ice_blocks):
        _, rows, cols = old_velocity.shape
        nbi, nbj = rows // BS, cols // BS
        nl, long = nbj + 1, rows + 2 * DEPTH
        vmem = pl.BlockSpec(memory_space=pltpu.VMEM)
        f32 = jnp.float32
        n_col = n_chip * n_grp
        dma = pltpu.SemaphoreType.DMA
        return pl.pallas_call(
            functools.partial(kernel, (n_chip, n_row, n_grp, rows, cols)),
            out_shape=jax.ShapeDtypeStruct(old_velocity.shape, f32),
            in_specs=[pl.BlockSpec(memory_space=pl.ANY)] * 7 + [pl.BlockSpec(memory_space=pltpu.SMEM)],
            out_specs=vmem,
            scratch_shapes=[
                pltpu.VMEM(old_velocity.shape, f32),
                pltpu.VMEM(old_velocity.shape, f32),
                pltpu.VMEM((rows, cols), f32),
                pltpu.VMEM((rows, cols), f32),
                pltpu.VMEM((rows, cols), f32),
                pltpu.VMEM((rows, cols), jnp.int32),
                pltpu.VMEM((rows, cols), jnp.int32),
                pltpu.VMEM((FIELDS, nl, long + 2 * PAD, BS), f32),
                pltpu.VMEM((STEPS, 2, nl, long + 2 * PAD, BS), f32),
                pltpu.VMEM((STEPS, 2, nl, long, BS), f32),
                pltpu.VMEM((2, nl, long + (nbi + 3) * PAD, BS), f32),
                pltpu.VMEM((2, nl, long + (nbi + 3) * PAD, BS), f32),
                pltpu.VMEM((4, nl, long, BS), f32),
                pltpu.VMEM((2, FIELDS, rows // PACKED, BS), f32),
                pltpu.VMEM((2, FIELDS, rows // PACKED, BS), f32),
                pltpu.VMEM((4, DEPTH, BS), f32),
                pltpu.VMEM((4, DEPTH, BS), f32),
                pltpu.VMEM((COUNT, BS), f32),
                pltpu.VMEM((COUNT, BS), f32),
                pltpu.VMEM((n_row - 1, COUNT, BS), f32),
                pltpu.VMEM((n_col - 1, COUNT, BS), f32),
                dma((7,)),
                dma((len(DIRS),)),
                dma((len(DIRS),)),
                dma((n_row - 1,)),
                dma((n_row - 1,)),
                dma((n_col - 1,)),
                dma((n_col - 1,)),
            ],
            compiler_params=pltpu.CompilerParams(
                collective_id=0, has_side_effects=True, vmem_limit_bytes=60 * 1024 * 1024
            ),
        )(old_velocity, surface_stress, mass_term, ocean_drag, strength, ice_mask, ocean_mask, ice_blocks)

    return jax.shard_map(
        shards,
        mesh=mesh,
        in_specs=(
            P(None, "row", ("chip", "grp")),
            P(None, "row", ("chip", "grp")),
            P("row", ("chip", "grp")),
            P("row", ("chip", "grp")),
            P("row", ("chip", "grp")),
            P("row", ("chip", "grp")),
            P("row", ("chip", "grp")),
            P(("chip", "grp"), None),
        ),
        out_specs=P(None, "row", ("chip", "grp")),
        check_vma=False,
    )
```
